256 devices in a mesh: section: 32 (over y, z_lo, core), tp: 8 (over z_hi, x).
Axes of the slice: x: 4, y: 4, z: 8 (z_hi: 2, z_lo: 4; z = z_hi * 4 + z_lo), core: 2. Of those that a mesh axis runs over, the one named last changes fastest.
Arguments:
- held_rows: bfloat16 [32, 256, 4096], P('section', 'tp'), may hold values from -17 to 17
- entering: bfloat16 [3, 256, 4096], P(None, 'tp'), may hold values from -17 to 17
- norm_gain: bfloat16 [32, 4096], P('section'), may hold values from 0.099609375 to 1.8984375
- w_query: bfloat16 [32, 4096, 4096], P('section', None, 'tp'), may hold values from -0.09375 to 0.09375
- b_query: bfloat16 [32, 4096], P('section', 'tp'), may hold values from -8 to 8
- w_keyval: bfloat16 [32, 4096, 2048], P('section', None, 'tp'), may hold values from -0.09375 to 0.09375
- b_keyval: bfloat16 [32, 2048], P('section', 'tp'), may hold values from -3 to 3
- w_out: bfloat16 [32, 4096, 4096], P('section', 'tp'), may hold values from -0.09375 to 0.09375
- prefix_keys: bfloat16 [32, 4, 512, 1024], P('section', None, None, 'tp'), may hold values from -8 to 8
- prefix_values: bfloat16 [32, 4, 512, 1024], P('section', None, None, 'tp'), may hold values from -5 to 5
- lengths: int32 [35], replicated, may hold values from 128 to 512, as said below
Outputs:
- leaving: bfloat16 [32, 256, 4096], P('section', 'tp')
- new_cache: bfloat16 [32, 4, 256, 2048], P('section', None, None, 'tp')
The draws below stay inside these ranges and needn't reach their ends.
Inputs may be any that keep to these rules, and one draw needn't show every extreme that they name: `lengths`: some block sees all 512 cached slots.
All inputs are finite; a program needn't handle non-finite values.
Results may differ from the reference program's by a relative error of at most 0.022.
Values may be sent and summed in bfloat16 or wider, within the bound.
A program may use at most 64 MiB of HBM per device.

```python
import math
import jax
import jax.numpy as jnp
from jax import lax

D = 4096
HEADS = 32
KV_HEADS = 8
HEAD_DIM = 128
BLOCK = 256
BLOCKS = 4
PREFIX = 512
SECTIONS = 32
GROUPS = 8


def residual_rows(key, array_shape):
    noise_key = jax.random.fold_in(key, 0)
    return jax.random.truncated_normal(noise_key, -4.0, 4.0, array_shape).astype(jnp.bfloat16)


def draw_held_rows(key, part):
    key = jax.random.fold_in(key, 1)
    return residual_rows(key, (SECTIONS, BLOCK, D))


def draw_entering(key, part):
    key = jax.random.fold_in(key, 5)
    return residual_rows(key, (BLOCKS - 1, BLOCK, D))


def draw_b_query(key, part):
    key = jax.random.fold_in(key, 2)
    base_part = 0.5 * jax.random.truncated_normal(key, -4.0, 4.0, (SECTIONS, HEADS * HEAD_DIM))
    return base_part.astype(jnp.bfloat16)


def draw_prefix_keys(key, part):
    key = jax.random.fold_in(key, 3)
    base_part = jax.random.truncated_normal(key, -4.0, 4.0, (SECTIONS, BLOCKS, PREFIX, KV_HEADS * HEAD_DIM))
    return base_part.astype(jnp.bfloat16)


def draw_lengths(key, part):
    key = jax.random.fold_in(key, 4)
    length_count = SECTIONS + BLOCKS - 1
    value_key, place_key = jax.random.split(key)
    drawn = jax.random.randint(value_key, (length_count,), PREFIX // 4, PREFIX + 1)
    place_index = jax.random.randint(place_key, (), 0, length_count)
    return jnp.where(jnp.arange(length_count, dtype=jnp.int32) == place_index, PREFIX, drawn).astype(jnp.int32)


def block_scale(rng, dims, cuts, low, largest):
    level, own = 1.0, jax.random.fold_in(rng, 6)
    for axis_at, blocks in cuts:
        draws = jnp.exp(jax.random.uniform(jax.random.fold_in(own, axis_at), (blocks,), jnp.float32, low / len(cuts), largest / len(cuts)))
        level = level * jnp.repeat(draws, dims[axis_at] // blocks).reshape([-1 if axis == axis_at else 1 for axis in range(len(dims))])
    return level


def centred(rng, dims, deviation, most, pieces=(), held_as=jnp.bfloat16):
    gain = block_scale(rng, dims, pieces, -0.22, 0.18) if pieces else 1.0
    result = jax.random.normal(rng, dims, jnp.float32) * deviation * gain
    return jnp.minimum(jnp.maximum(result, -most), most).astype(held_as)


def setup_inputs(seed: int = 0) -> dict:
    seeds = jax.random.split(jax.random.key(seed), 12)
    return {
        "held_rows": draw_held_rows(jax.random.fold_in(seeds[11], 71), 0),
        "entering": draw_entering(jax.random.fold_in(seeds[11], 71), 0),
        "norm_gain": jnp.clip(1.0 + 0.18 * jax.random.normal(seeds[2], (SECTIONS, D), jnp.float32), 0.099609375, 1.8984375).astype(jnp.bfloat16),
        "w_query": centred(seeds[3], (SECTIONS, D, HEADS * HEAD_DIM), D ** -0.5, 0.09375, ((0, 32), (2, 8))),
        "b_query": draw_b_query(jax.random.fold_in(seeds[11], 71), 0),
        "w_keyval": centred(seeds[5], (SECTIONS, D, 2 * KV_HEADS * HEAD_DIM), D ** -0.5, 0.09375, ((0, 32), (2, 8))),
        "b_keyval": centred(seeds[6], (SECTIONS, 2 * KV_HEADS * HEAD_DIM), 0.5, 3.0, ((0, 32), (1, 8))),
        "w_out": centred(seeds[7], (SECTIONS, HEADS * HEAD_DIM, D), (HEADS * HEAD_DIM) ** -0.5, 0.09375, ((0, 32), (1, 8))),
        "prefix_keys": draw_prefix_keys(jax.random.fold_in(seeds[11], 71), 0),
        "prefix_values": centred(seeds[9], (SECTIONS, BLOCKS, PREFIX, KV_HEADS * HEAD_DIM), 1.0, 5.0, ((0, 32), (3, 8))),
        "lengths": draw_lengths(jax.random.fold_in(seeds[11], 71), 0),
    }


rope_base = 1000000.0
norm_eps = 1e-06

def normalize(row_block, gain_row):
    widened = row_block.astype(jnp.float32)
    mean_square = lax.optimization_barrier(jnp.mean(widened * widened, axis=-1, keepdims=True))
    return (widened * lax.rsqrt(mean_square + norm_eps) * gain_row.astype(jnp.float32)).astype(jnp.bfloat16)

def rotate(vectors, positions):
    half_dim = vectors.shape[-1] // 2
    frequency = jnp.exp(-(jnp.arange(half_dim, dtype=jnp.float32) * 2.0 / vectors.shape[-1]) * math.log(rope_base))
    angles = positions[:, None] * frequency[None, :]
    cosine = jnp.cos(angles)[:, None, :]
    sine_part = jnp.sin(angles)[:, None, :]
    first_half = vectors[..., :half_dim]
    second_half = vectors[..., half_dim:]
    return jnp.concatenate([first_half * cosine - second_half * sine_part, second_half * cosine + first_half * sine_part], axis=-1)

def attend(projected, cached_keys, cached_values, offset, query_heads, key_heads, head_dim):
    row_count = projected.shape[0]
    slot_count = cached_keys.shape[0]
    query_cols = query_heads * head_dim
    queries = projected[:, :query_cols].reshape(row_count, query_heads, head_dim)
    key_value = projected[:, query_cols:].reshape(row_count, key_heads, 2, head_dim)
    positions = (offset + jnp.arange(row_count, dtype=jnp.int32)).astype(jnp.float32)
    turned_query = rotate(queries, positions).astype(jnp.bfloat16)
    turned_keys = rotate(key_value[:, :, 0], positions).astype(jnp.bfloat16)
    value_part = key_value[:, :, 1].astype(jnp.bfloat16)
    block_cache = jnp.stack([turned_keys, value_part], axis=2).reshape(row_count, key_heads * 2 * head_dim)
    key_rows = jnp.concatenate([cached_keys.reshape(slot_count, key_heads, head_dim), turned_keys], axis=0)
    value_rows = jnp.concatenate([cached_values.reshape(slot_count, key_heads, head_dim), value_part], axis=0)
    grouped = turned_query.reshape(row_count, key_heads, query_heads // key_heads, head_dim)
    scores = jnp.einsum('qkgd,skd->kgqs', grouped.astype(jnp.float32), key_rows.astype(jnp.float32), precision=lax.Precision.HIGHEST) * head_dim ** (-0.5)
    slot_index = jnp.arange(slot_count + row_count, dtype=jnp.int32)
    row_index = jnp.arange(row_count, dtype=jnp.int32)
    allowed = jnp.where(slot_index[None, :] < slot_count, slot_index[None, :] < offset, slot_index[None, :] - slot_count <= row_index[:, None])
    scores = jnp.where(allowed, scores, jnp.float32(-1e+30))
    top_score = lax.optimization_barrier(jnp.max(scores, axis=-1, keepdims=True))
    weights = jnp.exp(scores - top_score)
    softmax_weights = (weights / lax.optimization_barrier(jnp.sum(weights, axis=-1, keepdims=True))).astype(jnp.bfloat16)
    attended = jnp.einsum('kgqs,skd->qkgd', softmax_weights.astype(jnp.float32), value_rows.astype(jnp.float32), precision=lax.Precision.HIGHEST)
    return (block_cache, attended.reshape(row_count, query_heads * head_dim).astype(jnp.bfloat16))

def reference(held_rows, entering, norm_gain, w_query, b_query, w_keyval, b_keyval, w_out, prefix_keys, prefix_values, lengths):

    def one_section(carried, inputs):
        section_id, held_block, gain_row, query_weight, query_bias, keyval_weight, keyval_bias, out_weight, section_keys, section_values = inputs
        incoming = jnp.concatenate([held_block[None], carried], axis=0)
        outputs = []
        caches = []
        for step_index in range(BLOCKS):
            current = incoming[step_index]
            offset = lax.dynamic_index_in_dim(lengths, step_index - section_id + SECTIONS - 1, keepdims=False)
            normed = normalize(current, gain_row)
            projected = jnp.concatenate([jnp.dot(normed, query_weight, preferred_element_type=jnp.float32) + query_bias.astype(jnp.float32), jnp.dot(normed, keyval_weight, preferred_element_type=jnp.float32) + keyval_bias.astype(jnp.float32)], axis=1)
            block_cache, attended = attend(projected, section_keys[step_index], section_values[step_index], offset, HEADS, KV_HEADS, HEAD_DIM)
            head_blocks = attended.reshape(BLOCK, GROUPS, HEADS * HEAD_DIM // GROUPS).astype(jnp.float32)
            out_blocks = out_weight.reshape(GROUPS, HEADS * HEAD_DIM // GROUPS, D).astype(jnp.float32)
            partial_value = jnp.einsum('rnc,ncd->nrd', head_blocks, out_blocks, precision=lax.Precision.HIGHEST).astype(jnp.bfloat16)
            summed = lax.optimization_barrier(jnp.sum(partial_value.astype(jnp.float32), axis=0))
            output = (current.astype(jnp.float32) + summed).astype(jnp.bfloat16)
            outputs.append(output)
            caches.append(block_cache)
        passed = jnp.stack(outputs[:-1], axis=0)
        return (passed, (outputs[-1], jnp.stack(caches, axis=0)))
    section_ids = jnp.arange(SECTIONS, dtype=jnp.int32)
    unused, results = lax.scan(one_section, entering, (section_ids, held_rows, norm_gain, w_query, b_query, w_keyval, b_keyval, w_out, prefix_keys, prefix_values))
    return (results[0], results[1])
```

```python
import functools

import jax
import jax.numpy as jnp
import numpy as np
from jax import lax
from jax.experimental import pallas as pl
from jax.experimental.pallas import tpu as pltpu
from jax.sharding import PartitionSpec as P

MESH = pl.DeviceIdType.MESH
HEAD_DIM = 128
ROPE_BASE = 1000000.0
NORM_EPS = 1e-06
XN = 4
CHUNKS = 4


def relay_kernel(
    dims,
    lengths_ref,
    held_ref,
    entering_ref,
    gain_ref,
    wq_hbm,
    bq_ref,
    wkv_hbm,
    bkv_ref,
    wo_hbm,
    pk_hbm,
    pv_hbm,
    freq_ref,
    cosi_ref,
    sini_ref,
    leaving_ref,
    cache_ref,
    wq,
    wkv,
    wo,
    pk,
    pv,
    xb,
    part,
    rsr,
    zs,
    zr,
    fin,
    load_sem,
    gx_send,
    gx_recv,
    gz_send,
    gz_recv,
    rs_send,
    rs_recv,
    z_send,
    z_recv,
    ag_send,
    ag_recv,
    f_send,
    f_recv,
):
    sections, steps, block, width, shard, prefix, q_heads = dims
    chunk = block // CHUNKS
    piece = chunk // XN
    tiles = steps * CHUNKS
    s = lax.axis_index("section")
    t = lax.axis_index("tp")
    x = lax.rem(t, XN)
    z = t // XN
    nxt = lax.rem(s + 1, sections)
    prv = lax.rem(s + sections - 1, sections)

    def x_peer(d):
        return (s, z * XN + lax.rem(x + d, XN))

    def x_from(d):
        return lax.rem(x + XN - d, XN)

    z_peer = (s, lax.rem(t + XN, 2 * XN))
    z_peer_t = lax.rem(t + XN, 2 * XN)

    loads = [
        pltpu.make_async_copy(src, dst, load_sem.at[n])
        for n, (src, dst) in enumerate(
            [(wq_hbm, wq), (wkv_hbm, wkv), (pk_hbm, pk), (pv_hbm, pv), (wo_hbm, wo)]
        )
    ]
    own = pltpu.make_async_copy(
        held_ref, xb.at[0, pl.ds(pl.multiple_of(t * shard, shard), shard)], load_sem.at[5]
    )
    for copy in loads:
        copy.start()
    own.start()

    barrier = pltpu.get_barrier_semaphore()
    for d in range(1, 2 * XN):
        pl.semaphore_signal(
            barrier, inc=1, device_id=(s, lax.rem(t + d, 2 * XN)), device_id_type=MESH
        )
    for other in (nxt, prv):
        for zz in range(2):
            pl.semaphore_signal(
                barrier, inc=1, device_id=(other, zz * XN + x), device_id_type=MESH
            )
    pl.semaphore_wait(barrier, 2 * XN - 1 + 4)

    def remote(src, dst, send, recv, device):
        return pltpu.make_async_remote_copy(
            src_ref=src,
            dst_ref=dst,
            send_sem=send,
            recv_sem=recv,
            device_id=device,
            device_id_type=MESH,
        )

    def shard_rows(w, member):
        return xb.at[w, pl.ds(pl.multiple_of(member * shard, shard), shard)]

    def gather_x(w, src, plane, member, d):
        return remote(
            src,
            shard_rows(w, member),
            gx_send.at[w, plane, d - 1],
            gx_recv.at[w, plane, d - 1],
            x_peer(d),
        )

    def gather_first(w, src):
        remote(src, shard_rows(w, t), gz_send.at[w], gz_recv.at[w], z_peer).start()
        for d in (1, 3, 2):
            gather_x(w, src, 0, t, d).start()

    def gather_second(w, src):
        remote(src, shard_rows(w, z_peer_t), gz_send.at[w], gz_recv.at[w], z_peer).wait_recv()
        for d in (1, 3, 2):
            gather_x(w, shard_rows(w, z_peer_t), 1, z_peer_t, d).start()

    def gather_arrived(w, c):
        for h in range(2):
            member = 2 * c + h
            xs = lax.rem(member, XN)
            d = lax.rem(x + XN - xs, XN)
            plane = lax.rem(member // XN + z, 2)

            @pl.when(d > 0)
            def _():
                rows = shard_rows(w, member)
                remote(
                    rows,
                    rows,
                    gx_send.at[w, plane, d - 1],
                    gx_recv.at[w, plane, d - 1],
                    (s, t),
                ).wait_recv()

    def gather_sent(w, src):
        remote(src, shard_rows(w, t), gz_send.at[w], gz_recv.at[w], z_peer).wait_send()
        for d in (1, 3, 2):
            gather_x(w, src, 0, t, d).wait_send()
            gather_x(w, shard_rows(w, z_peer_t), 1, z_peer_t, d).wait_send()

    def piece_rows(w, c, owner):
        return xb.at[w, pl.ds(pl.multiple_of(c * chunk + owner * piece, piece), piece)]

    def part_rows(k, owner):
        return part.at[k, pl.ds(pl.multiple_of(owner * piece, piece), piece)]

    def rs_copy(k, d):
        return remote(
            part_rows(k, lax.rem(x + d, XN)),
            rsr.at[k, d - 1],
            rs_send.at[k, d - 1],
            rs_recv.at[k, d - 1],
            x_peer(d),
        )

    def z_copy(k, zz):
        return remote(
            zs.at[k],
            zr.at[k, z],
            z_send.at[k, zz],
            z_recv.at[k, z],
            (nxt, zz * XN + x),
        )

    def ag_copy(k, d):
        rows = piece_rows(k // CHUNKS + 1, lax.rem(k, CHUNKS), x)
        return remote(rows, rows, ag_send.at[k, d - 1], ag_recv.at[k, d - 1], x_peer(d))

    def ag_arrived(k):
        for d in (1, 3, 2):
            rows = piece_rows(k // CHUNKS + 1, lax.rem(k, CHUNKS), x_from(d))
            remote(
                rows, rows, ag_send.at[k, d - 1], ag_recv.at[k, d - 1], x_peer(d)
            ).wait_recv()

    def compute(k):
        w = k // CHUNKS
        c = lax.rem(k, CHUNKS)
        offset = lengths_ref[w - s + sections - 1]
        first = pl.multiple_of(c * chunk, chunk)
        rows = xb[w, pl.ds(first, chunk), :].astype(jnp.float32)
        mean_square = jnp.sum(rows * rows, axis=-1, keepdims=True) * (1.0 / width)
        normed = (
            rows * lax.rsqrt(mean_square + NORM_EPS) * gain_ref[...].astype(jnp.float32)
        ).astype(jnp.bfloat16)
        query = jnp.dot(normed, wq[...], preferred_element_type=jnp.float32)
        query = query + bq_ref[...].astype(jnp.float32)
        keyval = jnp.dot(normed, wkv[...], preferred_element_type=jnp.float32)
        keyval = keyval + bkv_ref[...].astype(jnp.float32)

        base = offset.astype(jnp.float32) * freq_ref[0:1, :]
        cos_b, sin_b = jnp.cos(base), jnp.sin(base)
        cos_i = cosi_ref[pl.ds(first, chunk), :]
        sin_i = sini_ref[pl.ds(first, chunk), :]
        cosine = cos_b * cos_i - sin_b * sin_i
        sine = (sin_b * cos_i + cos_b * sin_i) * freq_ref[1:2, :]

        def turn(v):
            return (v * cosine + pltpu.roll(v, HEAD_DIM // 2, 1) * sine).astype(jnp.bfloat16)

        cache_ref[w, pl.ds(first, chunk), 0:HEAD_DIM] = turn(keyval[:, :HEAD_DIM])
        cache_ref[w, pl.ds(first, chunk), HEAD_DIM:] = keyval[:, HEAD_DIM:].astype(jnp.bfloat16)
        turned = jnp.concatenate(
            [turn(query[:, h * HEAD_DIM : (h + 1) * HEAD_DIM]) for h in range(q_heads)], axis=0
        )

        scale = HEAD_DIM ** (-0.5)
        nt = (((1,), (1,)), ((), ()))
        far = (
            lax.dot_general(turned, pk[w], nt, preferred_element_type=jnp.float32) * scale
        )
        near = (
            lax.dot_general(
                turned, cache_ref[w, :, 0:HEAD_DIM], nt, preferred_element_type=jnp.float32
            )
            * scale
        )
        far_slot = lax.broadcasted_iota(jnp.int32, far.shape, 1)
        near_slot = lax.broadcasted_iota(jnp.int32, near.shape, 1)
        near_row = lax.rem(lax.broadcasted_iota(jnp.int32, near.shape, 0), chunk) + first
        far = jnp.where(far_slot < offset, far, -1e30)
        near = jnp.where(near_slot <= near_row, near, -1e30)
        top = jnp.maximum(
            jnp.max(far, axis=-1, keepdims=True), jnp.max(near, axis=-1, keepdims=True)
        )
        far = jnp.exp(far - top)
        near = jnp.exp(near - top)
        total = jnp.sum(far, axis=-1, keepdims=True) + jnp.sum(near, axis=-1, keepdims=True)
        mixed = jnp.dot(far.astype(jnp.bfloat16), pv[w], preferred_element_type=jnp.float32)
        mixed = mixed + jnp.dot(
            near.astype(jnp.bfloat16),
            cache_ref[w, :, HEAD_DIM:],
            preferred_element_type=jnp.float32,
        )
        mixed = (mixed / total).astype(jnp.bfloat16)
        attended = jnp.concatenate(
            [mixed[h * chunk : (h + 1) * chunk] for h in range(q_heads)], axis=1
        )
        part[k] = jnp.dot(attended, wo[...], preferred_element_type=jnp.float32).astype(
            jnp.bfloat16
        )

    def stage_one(k):
        w = k // CHUNKS
        c = lax.rem(k, CHUNKS)
        gathered = jnp.logical_or(s == 0, w == 0)

        @pl.when(gathered)
        def _():
            gather_arrived(w, c)

        @pl.when(jnp.logical_not(gathered))
        def _():
            ag_arrived(k - CHUNKS)

        compute(k)
        for d in (2, 1, 3):
            rs_copy(k, d).start()

    def stage_two(k):
        w = k // CHUNKS
        c = lax.rem(k, CHUNKS)
        for d in (1, 3, 2):
            rs_copy(k, d).wait_recv()
        rows = pl.ds(pl.multiple_of(c * chunk + x * piece, piece), piece)
        mine = xb[w, rows, :].astype(jnp.float32)
        summed = part[k, pl.ds(pl.multiple_of(x * piece, piece), piece), :].astype(jnp.float32)
        summed = summed + jnp.where(z == 0, mine, 0.0)
        for d in range(XN - 1):
            summed = summed + rsr[k, d].astype(jnp.float32)
        zs[k] = summed.astype(jnp.bfloat16)

        @pl.when(jnp.logical_and(w < steps - 1, s < sections - 1))
        def _():
            for zz in range(2):
                z_copy(k, zz).start()

        @pl.when(w == steps - 1)
        def _():
            owner = 2 * c + x // 2

            @pl.when(owner == t)
            def _():
                fin[z, lax.rem(x, 2)] = zs[k]

            @pl.when(owner != t)
            def _():
                remote(
                    zs.at[k],
                    fin.at[z, lax.rem(x, 2)],
                    f_send.at[c],
                    f_recv.at[z, lax.rem(x, 2)],
                    (s, owner),
                ).start()

        for d in (1, 3, 2):
            rs_copy(k, d).wait_send()

    def stage_three(k):
        for zz in range(2):
            remote(
                zs.at[k],
                zr.at[k, zz],
                z_send.at[k, zz],
                z_recv.at[k, zz],
                (nxt, zz * XN + x),
            ).wait_recv()
        w = k // CHUNKS
        c = lax.rem(k, CHUNKS)
        rows = pl.ds(pl.multiple_of(c * chunk + x * piece, piece), piece)
        xb[w + 1, rows, :] = (zr[k, 0].astype(jnp.float32) + zr[k, 1].astype(jnp.float32)).astype(
            jnp.bfloat16
        )
        for d in (2, 1, 3):
            ag_copy(k, d).start()

    gather_first(0, held_ref)
    cache_ref[...] = jnp.zeros_like(cache_ref)
    gather_second(0, held_ref)
    for copy in loads:
        copy.wait()
    own.wait()

    def body(i, carry):
        @pl.when(i < tiles)
        def _():
            stage_one(i)

        @pl.when(jnp.logical_and(i >= 1, i < tiles + 1))
        def _():
            stage_two(i - 1)

        inner = jnp.logical_and(i >= 2, i < tiles - CHUNKS + 2)

        @pl.when(jnp.logical_and(inner, s > 0))
        def _():
            stage_three(i - 2)

        later = jnp.logical_and(i >= 3, i < tiles - CHUNKS + 3)

        @pl.when(jnp.logical_and(later, s > 0))
        def _():
            for d in (1, 3, 2):
                ag_copy(i - 3, d).wait_send()

        @pl.when(jnp.logical_and(later, s < sections - 1))
        def _():
            for zz in range(2):
                z_copy(i - 3, zz).wait_send()

        entry = jnp.logical_and(s == 0, i < tiles - CHUNKS)
        w_in = i // CHUNKS
        src = entering_ref.at[w_in]

        @pl.when(jnp.logical_and(entry, lax.rem(i, CHUNKS) == 0))
        def _():
            keep = pltpu.make_async_copy(src, shard_rows(w_in + 1, t), load_sem.at[5])
            keep.start()
            gather_first(w_in + 1, src)
            keep.wait()

        @pl.when(jnp.logical_and(entry, lax.rem(i, CHUNKS) == 2))
        def _():
            gather_second(w_in + 1, src)

        @pl.when(jnp.logical_and(entry, lax.rem(i, CHUNKS) == 3))
        def _():
            gather_sent(w_in + 1, src)

        return carry

    lax.fori_loop(0, tiles + 1, body, 0)
    gather_sent(0, held_ref)

    for zz in range(2):
        for h in range(2):
            source = zz * XN + 2 * lax.rem(t, 2) + h

            @pl.when(source != t)
            def _():
                remote(
                    zs.at[0], fin.at[zz, h], f_send.at[0], f_recv.at[zz, h], (s, t)
                ).wait_recv()

    for h in range(2):
        leaving_ref[h * piece : (h + 1) * piece, :] = (
            fin[0, h].astype(jnp.float32) + fin[1, h].astype(jnp.float32)
        ).astype(jnp.bfloat16)
    for c in range(CHUNKS):

        @pl.when(2 * c + x // 2 != t)
        def _():
            remote(
                zs.at[0], fin.at[z, lax.rem(x, 2)], f_send.at[c], f_recv.at[0, 0], (s, t)
            ).wait_send()


def shards(
    held_rows,
    entering,
    norm_gain,
    w_query,
    b_query,
    w_keyval,
    b_keyval,
    w_out,
    prefix_keys,
    prefix_values,
    lengths,
):
    sections = lax.axis_size("section")
    _, shard, width = held_rows.shape
    _, steps, prefix, head_dim = prefix_keys.shape
    members = lax.axis_size("tp")
    block = shard * members
    q_cols = w_query.shape[2]
    kv_cols = w_keyval.shape[2]
    q_heads = q_cols // HEAD_DIM
    tiles = steps * CHUNKS
    piece = block // CHUNKS // XN
    half = HEAD_DIM // 2

    freq = np.exp(-(np.arange(half, dtype=np.float32) * 2.0 / HEAD_DIM) * np.log(ROPE_BASE))
    freq = np.concatenate([freq, freq]).astype(np.float32)
    sign = np.concatenate([-np.ones(half), np.ones(half)]).astype(np.float32)
    angles = np.arange(block, dtype=np.float64)[:, None] * freq[None, :].astype(np.float64)
    freq_sign = np.stack([freq, sign] + [np.zeros_like(freq)] * 6)

    bf16 = jnp.bfloat16
    vmem = pl.BlockSpec(memory_space=pltpu.VMEM)
    hbm = pl.BlockSpec(memory_space=pl.ANY)
    smem = pl.BlockSpec(memory_space=pltpu.SMEM)
    dma = pltpu.SemaphoreType.DMA
    inner = tiles - CHUNKS
    leaving, cache = pl.pallas_call(
        functools.partial(
            relay_kernel, (sections, steps, block, width, shard, prefix, q_heads)
        ),
        out_shape=(
            jax.ShapeDtypeStruct((shard, width), bf16),
            jax.ShapeDtypeStruct((steps, block, kv_cols), bf16),
        ),
        in_specs=[smem, hbm, hbm, vmem, hbm, vmem, hbm, vmem, hbm, hbm, hbm, vmem, vmem, vmem],
        out_specs=(vmem, vmem),
        scratch_shapes=[
            pltpu.VMEM((width, q_cols), bf16),
            pltpu.VMEM((width, kv_cols), bf16),
            pltpu.VMEM((q_cols, width), bf16),
            pltpu.VMEM((steps, prefix, head_dim), bf16),
            pltpu.VMEM((steps, prefix, head_dim), bf16),
            pltpu.VMEM((steps, block, width), bf16),
            pltpu.VMEM((tiles, block // CHUNKS, width), bf16),
            pltpu.VMEM((tiles, XN - 1, piece, width), bf16),
            pltpu.VMEM((tiles, piece, width), bf16),
            pltpu.VMEM((inner, 2, piece, width), bf16),
            pltpu.VMEM((2, 2, piece, width), bf16),
            dma((6,)),
            dma((steps, 2, XN - 1)),
            dma((steps, 2, XN - 1)),
            dma((steps,)),
            dma((steps,)),
            dma((tiles, XN - 1)),
            dma((tiles, XN - 1)),
            dma((inner, 2)),
            dma((inner, 2)),
            dma((inner, XN - 1)),
            dma((inner, XN - 1)),
            dma((CHUNKS,)),
            dma((2, 2)),
        ],
        compiler_params=pltpu.CompilerParams(
            collective_id=0, has_side_effects=True, vmem_limit_bytes=56 * 2**20
        ),
    )(
        lengths,
        held_rows[0],
        entering,
        norm_gain,
        w_query[0],
        b_query,
        w_keyval[0],
        b_keyval,
        w_out[0],
        prefix_keys[0],
        prefix_values[0],
        jnp.asarray(freq_sign, jnp.float32),
        jnp.asarray(np.cos(angles), jnp.float32),
        jnp.asarray(np.sin(angles), jnp.float32),
    )
    return (leaving[None], cache[None])


def solution(mesh):
    return jax.shard_map(
        shards,
        mesh=mesh,
        in_specs=(
            P("section", "tp", None),
            P(None, "tp", None),
            P("section", None),
            P("section", None, "tp"),
            P("section", "tp"),
            P("section", None, "tp"),
            P("section", "tp"),
            P("section", "tp", None),
            P("section", None, None, "tp"),
            P("section", None, None, "tp"),
            P(),
        ),
        out_specs=(P("section", "tp", None), P("section", None, None, "tp")),
        check_vma=False,
    )
```

```python
import functools

import jax
import jax.numpy as jnp
import numpy as np
from jax import lax
from jax.experimental import pallas as pl
from jax.experimental.pallas import tpu as pltpu
from jax.sharding import PartitionSpec as P

MESH = pl.DeviceIdType.MESH
HEAD_DIM = 128
ROPE_BASE = 1000000.0
NORM_EPS = 1e-06
XN = 4
CHUNKS = 8
SLOTS = 8
ORDER = (("compute", 0), ("attend", 0), ("relay", 1), ("forward", 6), ("z", 4), ("sum", 2), ("sent", 7))


def relay_kernel(
    dims,
    lengths_ref,
    held_ref,
    entering_ref,
    gain_ref,
    wq_hbm,
    bq_ref,
    wkv_hbm,
    bkv_ref,
    wo_hbm,
    pk_hbm,
    pv_hbm,
    freq_ref,
    cosi_ref,
    sini_ref,
    leaving_ref,
    cache_ref,
    wq,
    wkv,
    wo,
    pk,
    pv,
    xb,
    part,
    relay,
    rsr,
    zs,
    zr,
    fin,
    base,
    turned_ref,
    load_sem,
    gz_send,
    gz_recv,
    g1_send,
    g1_recv,
    g2_send,
    g2_recv,
    rs1_send,
    rs1_recv,
    rs2_send,
    rs2_recv,
    z_send,
    z_recv,
    ag1_send,
    ag1_recv,
    ag2_send,
    ag2_recv,
    f_send,
    f_recv,
):
    sections, steps, block, width, shard, q_heads = dims
    chunk = block // CHUNKS
    half = chunk // 2
    unit = shard // 2
    cols = width // XN
    tiles = steps * CHUNKS
    inner = tiles - CHUNKS
    s = lax.axis_index("section")
    t = lax.axis_index("tp")
    x = lax.rem(t, XN)
    z = t // XN
    nxt = lax.rem(s + 1, sections)
    prv = lax.rem(s + sections - 1, sections)
    at = [lax.rem(x + d, XN) for d in range(XN)]
    step_to = [(s, z * XN + at[1]), (s, z * XN + at[3])]
    came_from = [at[3], at[1]]
    tz = lax.rem(t + XN, 2 * XN)
    z_peer = (s, tz)

    def remote(src, dst, send, recv, device):
        return pltpu.make_async_remote_copy(
            src_ref=src,
            dst_ref=dst,
            send_sem=send,
            recv_sem=recv,
            device_id=device,
            device_id_type=MESH,
        )

    def arrived(ref, recv):
        remote(ref, ref, f_send.at[0], recv, (s, t)).wait_recv()

    def sent(ref, send):
        remote(ref, ref, send, f_recv.at[0, 0], (s, t)).wait_send()

    def ds(start, size):
        return pl.ds(pl.multiple_of(start, size), size)

    loads = [
        pltpu.make_async_copy(src, dst, load_sem.at[n])
        for n, (src, dst) in enumerate(
            [(wq_hbm, wq), (wkv_hbm, wkv), (pk_hbm, pk), (pv_hbm, pv), (wo_hbm, wo)]
        )
    ]

    barrier = pltpu.get_barrier_semaphore()
    for d in range(1, 2 * XN):
        pl.semaphore_signal(
            barrier, inc=1, device_id=(s, lax.rem(t + d, 2 * XN)), device_id_type=MESH
        )
    for other in (nxt, prv):
        for zz in range(2):
            pl.semaphore_signal(
                barrier, inc=1, device_id=(other, zz * XN + x), device_id_type=MESH
            )
    own = pltpu.make_async_copy(held_ref, xb.at[0, ds(t * shard, shard)], load_sem.at[5])
    own.start()
    for copy in loads:
        copy.start()
    pl.semaphore_wait(barrier, 2 * XN - 1 + 4)

    def rows_of(w, member, u):
        return xb.at[w, ds(member * shard + u * unit, unit)]

    def plane_member(plane, position):
        return position + XN * (z if plane == 0 else 1 - z)

    def g_z(w, src, u):
        return remote(
            src.at[pl.ds(u * unit, unit)], rows_of(w, t, u), gz_send.at[w, u], gz_recv.at[w, u], z_peer
        )

    def g_near(w, src, plane, u, way):
        return remote(
            src,
            rows_of(w, plane_member(plane, x), u),
            g1_send.at[w, plane, u, way],
            g1_recv.at[w, plane, u, way],
            step_to[way],
        )

    def g_far(w, plane, u):
        rows = rows_of(w, plane_member(plane, came_from[u]), u)
        return remote(
            rows, rows, g2_send.at[w, plane, u], g2_recv.at[w, plane, u], step_to[u]
        )

    def gather_across(w, src):
        for u in range(2):
            g_z(w, src, u).start()

    def gather_first(w, src):
        for u in range(2):
            for way in range(2):
                g_near(w, src.at[pl.ds(u * unit, unit)], 0, u, way).start()

    def gather_relay(w, plane):
        for u in range(2):
            arrived(
                rows_of(w, plane_member(plane, came_from[u]), u), g1_recv.at[w, plane, u, u]
            )
            g_far(w, plane, u).start()

    def gather_z(w):
        for u in range(2):
            rows = rows_of(w, tz, u)
            arrived(rows, gz_recv.at[w, u])
            for way in range(2):
                g_near(w, rows, 1, u, way).start()

    def gather_chunk(w, c):
        for h in range(chunk // shard):
            member = c * (chunk // shard) + h
            plane = lax.rem(member // XN + z, 2)
            distance = lax.rem(x + XN - lax.rem(member, XN), XN)
            for u in range(2):
                rows = rows_of(w, member, u)

                @pl.when(distance == 1 + 2 * (1 - u))
                def _():
                    arrived(rows, g1_recv.at[w, plane, u, 1 - u])

                @pl.when(distance == 2)
                def _():
                    arrived(rows, g2_recv.at[w, plane, u])

    def gather_sent(w):
        for u in range(2):
            sent(rows_of(w, t, u), gz_send.at[w, u])
            for plane in range(2):
                for way in range(2):
                    sent(rows_of(w, t, u), g1_send.at[w, plane, u, way])
                sent(rows_of(w, t, u), g2_send.at[w, plane, u])

    upper, lower = pl.ds(0, half), pl.ds(half, half)
    halves = [upper, lower]

    def col(owner):
        return ds(owner * cols, cols)

    def slot(k):
        return lax.rem(k, SLOTS)

    def chunk_rows(c, h=None):
        if h is None:
            return ds(c * chunk, chunk)
        return ds(c * chunk + h * half, half)

    def prepare():
        turns = [
            lengths_ref[w - s + sections - 1].astype(jnp.float32) * freq_ref[0:1, :]
            for w in range(steps)
        ]
        base_angles = jnp.concatenate(turns + [turns[0]] * (8 - steps), axis=0)
        base[0] = jnp.cos(base_angles)
        base[1] = jnp.sin(base_angles)

    def project_in(k):
        w = k // CHUNKS
        c = lax.rem(k, CHUNKS)
        here = chunk_rows(c)
        rows = xb[w, here, :].astype(jnp.float32)
        mean_square = jnp.sum(rows * rows, axis=-1, keepdims=True) * (1.0 / width)
        normed = (
            rows * lax.rsqrt(mean_square + NORM_EPS) * gain_ref[...].astype(jnp.float32)
        ).astype(jnp.bfloat16)
        keyval = jnp.dot(normed, wkv[...], preferred_element_type=jnp.float32)
        keyval = keyval + bkv_ref[...].astype(jnp.float32)
        query = jnp.dot(normed, wq[...], preferred_element_type=jnp.float32)
        query = query + bq_ref[...].astype(jnp.float32)

        cos_b = base[0, pl.ds(w, 1), :]
        sin_b = base[1, pl.ds(w, 1), :]
        cos_i = cosi_ref[here, :]
        sin_i = sini_ref[here, :]
        cosine = cos_b * cos_i - sin_b * sin_i
        sine = (sin_b * cos_i + cos_b * sin_i) * freq_ref[1:2, :]

        def turn(v):
            return (v * cosine + pltpu.roll(v, HEAD_DIM // 2, 1) * sine).astype(jnp.bfloat16)

        cache_ref[w, here, 0:HEAD_DIM] = turn(keyval[:, :HEAD_DIM])
        cache_ref[w, here, HEAD_DIM:] = keyval[:, HEAD_DIM:].astype(jnp.bfloat16)
        for h in range(q_heads):
            turned_ref[h * chunk : (h + 1) * chunk, :] = turn(
                query[:, h * HEAD_DIM : (h + 1) * HEAD_DIM]
            )

    def attend(k):
        w = k // CHUNKS
        c = lax.rem(k, CHUNKS)
        offset = lengths_ref[w - s + sections - 1]
        turned = turned_ref[...]
        scale = HEAD_DIM ** (-0.5)
        nt = (((1,), (1,)), ((), ()))
        far = lax.dot_general(turned, pk[w], nt, preferred_element_type=jnp.float32) * scale
        near = (
            lax.dot_general(
                turned, cache_ref[w, :, 0:HEAD_DIM], nt, preferred_element_type=jnp.float32
            )
            * scale
        )
        far_slot = lax.broadcasted_iota(jnp.int32, far.shape, 1)
        near_slot = lax.broadcasted_iota(jnp.int32, near.shape, 1)
        near_row = lax.rem(lax.broadcasted_iota(jnp.int32, near.shape, 0), chunk) + c * chunk
        far = jnp.where(far_slot < offset, far, -1e30)
        near = jnp.where(near_slot <= near_row, near, -1e30)
        top = jnp.maximum(
            jnp.max(far, axis=-1, keepdims=True), jnp.max(near, axis=-1, keepdims=True)
        )
        far = jnp.exp(far - top)
        near = jnp.exp(near - top)
        total = jnp.sum(far, axis=-1, keepdims=True) + jnp.sum(near, axis=-1, keepdims=True)
        mixed = jnp.dot(far.astype(jnp.bfloat16), pv[w], preferred_element_type=jnp.float32)
        mixed = mixed + jnp.dot(
            near.astype(jnp.bfloat16),
            cache_ref[w, :, HEAD_DIM:],
            preferred_element_type=jnp.float32,
        )
        mixed = (mixed / total).astype(jnp.bfloat16)
        return jnp.concatenate(
            [mixed[h * chunk : (h + 1) * chunk] for h in range(q_heads)], axis=1
        )

    def rs_through(k, way):
        return remote(
            part.at[k, halves[way], col(at[2])],
            relay.at[k, way],
            rs1_send.at[slot(k), way, 0],
            rs1_recv.at[k, way, 0],
            step_to[way],
        )

    def rs_near(k, way):
        return remote(
            part.at[k, halves[1 - way], col(came_from[1 - way])],
            rsr.at[k, way, halves[1 - way]],
            rs1_send.at[slot(k), way, 1],
            rs1_recv.at[k, way, 1],
            step_to[way],
        )

    def rs_on(k, way):
        return remote(
            relay.at[k, way],
            rsr.at[k, way, halves[way]],
            rs2_send.at[slot(k), way],
            rs2_recv.at[k, way],
            step_to[way],
        )

    def z_copy(k, zz):
        return remote(
            zs.at[k],
            zr.at[k, z],
            z_send.at[slot(k), zz],
            z_recv.at[k, z],
            (nxt, zz * XN + x),
        )

    def ag_near(k, way):
        rows = xb.at[k // CHUNKS + 1, chunk_rows(lax.rem(k, CHUNKS)), col(x)]
        return remote(
            rows, rows, ag1_send.at[slot(k), way], ag1_recv.at[k, way], step_to[way]
        )

    def ag_far_rows(k, way, owner):
        return xb.at[k // CHUNKS + 1, chunk_rows(lax.rem(k, CHUNKS), way), col(owner)]

    def ag_far(k, way):
        rows = ag_far_rows(k, way, came_from[way])
        return remote(
            rows, rows, ag2_send.at[slot(k), way], ag2_recv.at[k, way], step_to[way]
        )

    def stage_compute(k):
        w = k // CHUNKS
        c = lax.rem(k, CHUNKS)
        gathered = jnp.logical_or(s == 0, w == 0)

        @pl.when(gathered)
        def _():
            gather_chunk(w, c)

        @pl.when(jnp.logical_not(gathered))
        def _():
            for way in range(2):
                arrived(ag_far_rows(k - CHUNKS, way, at[2]), ag2_recv.at[k - CHUNKS, way])

        project_in(k)

    def stage_attend(k):
        attended = attend(k)

        def project(owner):
            part[k, :, col(owner)] = jnp.dot(
                attended, wo[:, col(owner)], preferred_element_type=jnp.float32
            ).astype(jnp.bfloat16)

        project(at[2])
        for way in range(2):
            rs_through(k, way).start()
        project(at[1])
        rs_near(k, 0).start()
        project(at[3])
        rs_near(k, 1).start()
        project(x)

    def stage_relay(k):
        for way in range(2):
            arrived(relay.at[k, way], rs1_recv.at[k, way, 0])
            relay[k, way] = (
                relay[k, way].astype(jnp.float32)
                + part[k, halves[way], col(at[1 if way == 0 else 3])].astype(jnp.float32)
            ).astype(jnp.bfloat16)
            rs_on(k, way).start()

    def stage_sum(k):
        w = k // CHUNKS
        c = lax.rem(k, CHUNKS)
        for way in range(2):
            arrived(rsr.at[k, way, halves[1 - way]], rs1_recv.at[k, way, 1])
            arrived(rsr.at[k, way, halves[way]], rs2_recv.at[k, way])
        mine = xb[w, chunk_rows(c), col(x)].astype(jnp.float32)
        summed = part[k, :, col(x)].astype(jnp.float32) + jnp.where(z == 0, mine, 0.0)
        summed = summed + rsr[k, 0].astype(jnp.float32) + rsr[k, 1].astype(jnp.float32)
        zs[k] = summed.astype(jnp.bfloat16)

        @pl.when(jnp.logical_and(w < steps - 1, s < sections - 1))
        def _():
            for zz in (1 - z, z):
                z_copy(k, zz).start()

        @pl.when(w == steps - 1)
        def _():
            for h in range(chunk // shard):
                owner = c * (chunk // shard) + h
                rows = pl.ds(h * shard, shard)

                @pl.when(owner == t)
                def _():
                    fin[z, :, col(x)] = zs[k, rows, :]

                @pl.when(owner != t)
                def _():
                    remote(
                        zs.at[k, rows],
                        fin.at[z, :, col(x)],
                        f_send.at[owner],
                        f_recv.at[z, x],
                        (s, owner),
                    ).start()

    def stage_z(k):
        for zz in range(2):
            arrived(zr.at[k, zz], z_recv.at[k, zz])
        xb[k // CHUNKS + 1, chunk_rows(lax.rem(k, CHUNKS)), col(x)] = (
            zr[k, 0].astype(jnp.float32) + zr[k, 1].astype(jnp.float32)
        ).astype(jnp.bfloat16)
        for way in range(2):
            ag_near(k, way).start()

    def stage_forward(k):
        w = k // CHUNKS
        rows = chunk_rows(lax.rem(k, CHUNKS))
        for way in range(2):
            arrived(xb.at[w + 1, rows, col(came_from[way])], ag1_recv.at[k, way])
            ag_far(k, way).start()

    def stage_sent(k):
        for way in range(2):
            for n in range(2):
                sent(relay.at[k, way], rs1_send.at[slot(k), way, n])
            sent(relay.at[k, way], rs2_send.at[slot(k), way])

        @pl.when(jnp.logical_and(k < inner, s < sections - 1))
        def _():
            for zz in range(2):
                sent(zs.at[k], z_send.at[slot(k), zz])

        @pl.when(jnp.logical_and(k < inner, s > 0))
        def _():
            for way in range(2):
                sent(zs.at[k], ag1_send.at[slot(k), way])
                sent(relay.at[k, way], ag2_send.at[slot(k), way])

    @pl.when(z == 0)
    def _():
        gather_across(0, held_ref)

    gather_first(0, held_ref)
    cache_ref[...] = jnp.zeros_like(cache_ref)
    prepare()
    gather_relay(0, 0)

    @pl.when(z == 1)
    def _():
        gather_z(0)
        gather_across(0, held_ref)
        gather_relay(0, 1)

    for copy in loads:
        copy.wait()
    own.wait()

    def body(i, carry):
        def staged(after, count, stage, more=True):
            @pl.when(jnp.logical_and(jnp.logical_and(i >= after, i < after + count), more))
            def _():
                stage(i - after)

        calls = dict(
            compute=(tiles, stage_compute, True),
            attend=(tiles, stage_attend, True),
            relay=(tiles, stage_relay, True),
            sum=(tiles, stage_sum, True),
            z=(inner, stage_z, s > 0),
            forward=(inner, stage_forward, s > 0),
            sent=(tiles, stage_sent, True),
        )
        for name, after in ORDER:
            staged(after, *calls[name])

        entry = jnp.logical_and(s == 0, i < inner)
        w_in = i // CHUNKS
        src = entering_ref.at[w_in]

        @pl.when(jnp.logical_and(entry, lax.rem(i, CHUNKS) == 0))
        def _():
            keep = pltpu.make_async_copy(src, xb.at[w_in + 1, ds(t * shard, shard)], load_sem.at[5])
            keep.start()
            gather_across(w_in + 1, src)
            gather_first(w_in + 1, src)
            keep.wait()

        @pl.when(jnp.logical_and(entry, lax.rem(i, CHUNKS) == CHUNKS // 2))
        def _():
            gather_relay(w_in + 1, 0)
            gather_z(w_in + 1)

        @pl.when(jnp.logical_and(entry, lax.rem(i, CHUNKS) == CHUNKS - 2))
        def _():
            gather_relay(w_in + 1, 1)

        @pl.when(jnp.logical_and(z == 0, i == CHUNKS // 4 - 1))
        def _():
            gather_z(0)

        @pl.when(jnp.logical_and(z == 0, i == CHUNKS // 4))
        def _():
            gather_relay(0, 1)

        return carry

    lax.fori_loop(0, tiles + max(after for _, after in ORDER), body, 0)
    gather_sent(0)

    @pl.when(s == 0)
    def _():
        for w in range(1, steps):
            gather_sent(w)

    for zz in range(2):
        for xx in range(XN):

            @pl.when(zz * XN + xx != t)
            def _():
                arrived(fin.at[zz, :, pl.ds(xx * cols, cols)], f_recv.at[zz, xx])

    leaving_ref[...] = (fin[0].astype(jnp.float32) + fin[1].astype(jnp.float32)).astype(
        jnp.bfloat16
    )
    for owner in range(2 * XN):

        @pl.when(owner != t)
        def _():
            sent(fin.at[0, :, pl.ds(0, cols)], f_send.at[owner])


def shards(
    held_rows,
    entering,
    norm_gain,
    w_query,
    b_query,
    w_keyval,
    b_keyval,
    w_out,
    prefix_keys,
    prefix_values,
    lengths,
):
    sections = lax.axis_size("section")
    _, shard, width = held_rows.shape
    _, steps, prefix, head_dim = prefix_keys.shape
    members = lax.axis_size("tp")
    block = shard * members
    q_cols = w_query.shape[2]
    kv_cols = w_keyval.shape[2]
    q_heads = q_cols // HEAD_DIM
    tiles = steps * CHUNKS
    chunk = block // CHUNKS
    cols = width // XN
    half = HEAD_DIM // 2

    freq = np.exp(-(np.arange(half, dtype=np.float32) * 2.0 / HEAD_DIM) * np.log(ROPE_BASE))
    freq = np.concatenate([freq, freq]).astype(np.float32)
    sign = np.concatenate([-np.ones(half), np.ones(half)]).astype(np.float32)
    angles = np.arange(block, dtype=np.float64)[:, None] * freq[None, :].astype(np.float64)
    freq_sign = np.stack([freq, sign] + [np.zeros_like(freq)] * 6)

    bf16 = jnp.bfloat16
    vmem = pl.BlockSpec(memory_space=pltpu.VMEM)
    hbm = pl.BlockSpec(memory_space=pl.ANY)
    smem = pl.BlockSpec(memory_space=pltpu.SMEM)
    dma = pltpu.SemaphoreType.DMA
    inner = tiles - CHUNKS
    leaving, cache = pl.pallas_call(
        functools.partial(
            relay_kernel, (sections, steps, block, width, shard, q_heads)
        ),
        out_shape=(
            jax.ShapeDtypeStruct((shard, width), bf16),
            jax.ShapeDtypeStruct((steps, block, kv_cols), bf16),
        ),
        in_specs=[smem, hbm, hbm, vmem, hbm, vmem, hbm, vmem, hbm, hbm, hbm, vmem, vmem, vmem],
        out_specs=(vmem, vmem),
        scratch_shapes=[
            pltpu.VMEM((width, q_cols), bf16),
            pltpu.VMEM((width, kv_cols), bf16),
            pltpu.VMEM((q_cols, width), bf16),
            pltpu.VMEM((steps, prefix, head_dim), bf16),
            pltpu.VMEM((steps, prefix, head_dim), bf16),
            pltpu.VMEM((steps, block, width), bf16),
            pltpu.VMEM((tiles, chunk, width), bf16),
            pltpu.VMEM((tiles, 2, chunk // 2, cols), bf16),
            pltpu.VMEM((tiles, 2, chunk, cols), bf16),
            pltpu.VMEM((tiles, chunk, cols), bf16),
            pltpu.VMEM((inner, 2, chunk, cols), bf16),
            pltpu.VMEM((2, shard, width), bf16),
            pltpu.VMEM((2, 8, HEAD_DIM), jnp.float32),
            pltpu.VMEM((q_cols // HEAD_DIM * chunk, HEAD_DIM), bf16),
            dma((6,)),
            dma((steps, 2)),
            dma((steps, 2)),
            dma((steps, 2, 2, 2)),
            dma((steps, 2, 2, 2)),
            dma((steps, 2, 2)),
            dma((steps, 2, 2)),
            dma((SLOTS, 2, 2)),
            dma((tiles, 2, 2)),
            dma((SLOTS, 2)),
            dma((tiles, 2)),
            dma((SLOTS, 2)),
            dma((inner, 2)),
            dma((SLOTS, 2)),
            dma((inner, 2)),
            dma((SLOTS, 2)),
            dma((inner, 2)),
            dma((members,)),
            dma((2, XN)),
        ],
        compiler_params=pltpu.CompilerParams(
            collective_id=0, has_side_effects=True, vmem_limit_bytes=56 * 2**20
        ),
    )(
        lengths,
        held_rows[0],
        entering,
        norm_gain,
        w_query[0],
        b_query,
        w_keyval[0],
        b_keyval,
        w_out[0],
        prefix_keys[0],
        prefix_values[0],
        jnp.asarray(freq_sign, jnp.float32),
        jnp.asarray(np.cos(angles), jnp.float32),
        jnp.asarray(np.sin(angles), jnp.float32),
    )
    return (leaving[None], cache[None])


def solution(mesh):
    return jax.shard_map(
        shards,
        mesh=mesh,
        in_specs=(
            P("section", "tp", None),
            P(None, "tp", None),
            P("section", None),
            P("section", None, "tp"),
            P("section", "tp"),
            P("section", None, "tp"),
            P("section", "tp"),
            P("section", "tp", None),
            P("section", None, None, "tp"),
            P("section", None, None, "tp"),
            P(),
        ),
        out_specs=(P("section", "tp", None), P("section", None, None, "tp")),
        check_vma=False,
    )
```

```python
import functools

import jax
import jax.numpy as jnp
import numpy as np
from jax import lax
from jax.experimental import pallas as pl
from jax.experimental.pallas import tpu as pltpu
from jax.sharding import PartitionSpec as P

MESH = pl.DeviceIdType.MESH
HEAD_DIM = 128
ROPE_BASE = 1000000.0
NORM_EPS = 1e-06
XN = 4
CHUNKS = 8
SLOTS = 8
ORDER = (("relay", 2), ("compute", 0), ("z", 5), ("attend", 0), ("sum", 3), ("forward", 6), ("sent", 7))


def relay_kernel(
    dims,
    lengths_ref,
    held_ref,
    entering_ref,
    gain_ref,
    wq_hbm,
    bq_ref,
    wkv_hbm,
    bkv_ref,
    wo_hbm,
    pk_hbm,
    pv_hbm,
    freq_ref,
    cosi_ref,
    sini_ref,
    leaving_ref,
    cache_ref,
    wq,
    wkv,
    wo,
    pk,
    pv,
    xb,
    part,
    relay,
    rsr,
    zs,
    zr,
    fin,
    base,
    turned_ref,
    load_sem,
    gz_send,
    gz_recv,
    g1_send,
    g1_recv,
    g2_send,
    g2_recv,
    rs1_send,
    rs1_recv,
    rs2_send,
    rs2_recv,
    z_send,
    z_recv,
    ag1_send,
    ag1_recv,
    ag2_send,
    ag2_recv,
    f_send,
    f_recv,
):
    sections, steps, block, width, shard, q_heads = dims
    chunk = block // CHUNKS
    half = chunk // 2
    cols = width // XN
    tiles = steps * CHUNKS
    inner = tiles - CHUNKS
    s = lax.axis_index("section")
    t = lax.axis_index("tp")
    x = lax.rem(t, XN)
    z = t // XN
    nxt = lax.rem(s + 1, sections)
    prv = lax.rem(s + sections - 1, sections)
    at = [lax.rem(x + d, XN) for d in range(XN)]
    step_to = [(s, z * XN + at[1]), (s, z * XN + at[3])]
    came_from = [at[3], at[1]]
    tz = lax.rem(t + XN, 2 * XN)
    z_peer = (s, tz)

    def remote(src, dst, send, recv, device):
        return pltpu.make_async_remote_copy(
            src_ref=src,
            dst_ref=dst,
            send_sem=send,
            recv_sem=recv,
            device_id=device,
            device_id_type=MESH,
        )

    def arrived(ref, recv):
        remote(ref, ref, f_send.at[0], recv, (s, t)).wait_recv()

    def sent(ref, send):
        remote(ref, ref, send, f_recv.at[0, 0], (s, t)).wait_send()

    def ds(start, size):
        return pl.ds(pl.multiple_of(start, size), size)

    loads = [
        pltpu.make_async_copy(src, dst, load_sem.at[n])
        for n, (src, dst) in enumerate(
            [(wq_hbm, wq), (wkv_hbm, wkv), (pk_hbm, pk), (pv_hbm, pv), (wo_hbm, wo)]
        )
    ]

    barrier = pltpu.get_barrier_semaphore()
    for d in range(1, 2 * XN):
        pl.semaphore_signal(
            barrier, inc=1, device_id=(s, lax.rem(t + d, 2 * XN)), device_id_type=MESH
        )
    for other in (nxt, prv):
        for zz in range(2):
            pl.semaphore_signal(
                barrier, inc=1, device_id=(other, zz * XN + x), device_id_type=MESH
            )
    own = pltpu.make_async_copy(held_ref, xb.at[0, ds(t * shard, shard)], load_sem.at[5])
    own.start()
    for copy in loads:
        copy.start()
    pl.semaphore_wait(barrier, 2 * XN - 1 + 4)

    def rows_of(w, member, u):
        return xb.at[w, ds(member * shard, shard), pl.ds(u * cols, cols)]

    def plane_member(plane, position):
        return position + XN * (z if plane == 0 else 1 - z)

    def g_z(w, src, u):
        return remote(
            src.at[:, pl.ds(u * cols, cols)],
            rows_of(w, t, u),
            gz_send.at[w, u],
            gz_recv.at[w, u],
            z_peer,
        )

    def g_near(w, src, plane, u, way):
        return remote(
            src,
            rows_of(w, plane_member(plane, x), u),
            g1_send.at[w, plane, u, way],
            g1_recv.at[w, plane, u, way],
            step_to[way],
        )

    def g_far(w, plane, u):
        way = u % 2
        rows = rows_of(w, plane_member(plane, came_from[way]), u)
        return remote(
            rows, rows, g2_send.at[w, plane, u], g2_recv.at[w, plane, u], step_to[way]
        )

    def gather_across(w, src):
        for u in range(XN):
            g_z(w, src, u).start()

    def gather_first(w, src):
        for u in range(XN):
            for way in range(2):
                g_near(w, src.at[:, pl.ds(u * cols, cols)], 0, u, way).start()

    def relay_unit(w, plane, u):
        way = u % 2
        arrived(
            rows_of(w, plane_member(plane, came_from[way]), u), g1_recv.at[w, plane, u, way]
        )
        g_far(w, plane, u).start()

    def gather_relay(w, plane):
        for u in range(XN):
            relay_unit(w, plane, u)

    def z_unit(w, u):
        rows = rows_of(w, tz, u)
        arrived(rows, gz_recv.at[w, u])
        for way in range(2):
            g_near(w, rows, 1, u, way).start()

    def gather_z(w):
        for u in range(XN):
            z_unit(w, u)

    def gather_chunk(w, c):
        for h in range(chunk // shard):
            member = c * (chunk // shard) + h
            plane = lax.rem(member // XN + z, 2)
            distance = lax.rem(x + XN - lax.rem(member, XN), XN)
            for u in range(XN):
                rows = rows_of(w, member, u)
                other = 1 - u % 2

                @pl.when(distance == 1 + 2 * other)
                def _():
                    arrived(rows, g1_recv.at[w, plane, u, other])

                @pl.when(distance == 2)
                def _():
                    arrived(rows, g2_recv.at[w, plane, u])

    def gather_sent(w):
        for u in range(XN):
            sent(rows_of(w, t, u), gz_send.at[w, u])
            for plane in range(2):
                for way in range(2):
                    sent(rows_of(w, t, u), g1_send.at[w, plane, u, way])
                sent(rows_of(w, t, u), g2_send.at[w, plane, u])

    upper, lower = pl.ds(0, half), pl.ds(half, half)
    halves = [upper, lower]

    def col(owner):
        return ds(owner * cols, cols)

    def slot(k):
        return lax.rem(k, SLOTS)

    def chunk_rows(c, h=None):
        if h is None:
            return ds(c * chunk, chunk)
        return ds(c * chunk + h * half, half)

    def prepare():
        turns = [
            lengths_ref[w - s + sections - 1].astype(jnp.float32) * freq_ref[0:1, :]
            for w in range(steps)
        ]
        base_angles = jnp.concatenate(turns + [turns[0]] * (8 - steps), axis=0)
        base[0] = jnp.cos(base_angles)
        base[1] = jnp.sin(base_angles)

    def project_in(k):
        w = k // CHUNKS
        c = lax.rem(k, CHUNKS)
        here = chunk_rows(c)
        rows = xb[w, here, :].astype(jnp.float32)
        mean_square = jnp.sum(rows * rows, axis=-1, keepdims=True) * (1.0 / width)
        normed = (
            rows * lax.rsqrt(mean_square + NORM_EPS) * gain_ref[...].astype(jnp.float32)
        ).astype(jnp.bfloat16)
        keyval = jnp.dot(normed, wkv[...], preferred_element_type=jnp.float32)
        keyval = keyval + bkv_ref[...].astype(jnp.float32)
        query = jnp.dot(normed, wq[...], preferred_element_type=jnp.float32)
        query = query + bq_ref[...].astype(jnp.float32)

        cos_b = base[0, pl.ds(w, 1), :]
        sin_b = base[1, pl.ds(w, 1), :]
        cos_i = cosi_ref[here, :]
        sin_i = sini_ref[here, :]
        cosine = cos_b * cos_i - sin_b * sin_i
        sine = (sin_b * cos_i + cos_b * sin_i) * freq_ref[1:2, :]

        def turn(v):
            return (v * cosine + pltpu.roll(v, HEAD_DIM // 2, 1) * sine).astype(jnp.bfloat16)

        cache_ref[w, here, 0:HEAD_DIM] = turn(keyval[:, :HEAD_DIM])
        cache_ref[w, here, HEAD_DIM:] = keyval[:, HEAD_DIM:].astype(jnp.bfloat16)
        for h in range(q_heads):
            turned_ref[h * chunk : (h + 1) * chunk, :] = turn(
                query[:, h * HEAD_DIM : (h + 1) * HEAD_DIM]
            )

    def attend(k):
        w = k // CHUNKS
        c = lax.rem(k, CHUNKS)
        offset = lengths_ref[w - s + sections - 1]
        turned = turned_ref[...]
        scale = HEAD_DIM ** (-0.5)
        nt = (((1,), (1,)), ((), ()))
        far = lax.dot_general(turned, pk[w], nt, preferred_element_type=jnp.float32) * scale
        near = (
            lax.dot_general(
                turned, cache_ref[w, :, 0:HEAD_DIM], nt, preferred_element_type=jnp.float32
            )
            * scale
        )
        far_slot = lax.broadcasted_iota(jnp.int32, far.shape, 1)
        near_slot = lax.broadcasted_iota(jnp.int32, near.shape, 1)
        near_row = lax.rem(lax.broadcasted_iota(jnp.int32, near.shape, 0), chunk) + c * chunk
        far = jnp.where(far_slot < offset, far, -1e30)
        near = jnp.where(near_slot <= near_row, near, -1e30)
        top = jnp.maximum(
            jnp.max(far, axis=-1, keepdims=True), jnp.max(near, axis=-1, keepdims=True)
        )
        far = jnp.exp(far - top)
        near = jnp.exp(near - top)
        total = jnp.sum(far, axis=-1, keepdims=True) + jnp.sum(near, axis=-1, keepdims=True)
        mixed = jnp.dot(far.astype(jnp.bfloat16), pv[w], preferred_element_type=jnp.float32)
        mixed = mixed + jnp.dot(
            near.astype(jnp.bfloat16),
            cache_ref[w, :, HEAD_DIM:],
            preferred_element_type=jnp.float32,
        )
        mixed = (mixed / total).astype(jnp.bfloat16)
        return jnp.concatenate(
            [mixed[h * chunk : (h + 1) * chunk] for h in range(q_heads)], axis=1
        )

    def rs_through(k, way):
        return remote(
            part.at[k, halves[way], col(at[2])],
            relay.at[k, way],
            rs1_send.at[slot(k), way, 0],
            rs1_recv.at[k, way, 0],
            step_to[way],
        )

    def rs_near(k, way):
        return remote(
            part.at[k, halves[1 - way], col(came_from[1 - way])],
            rsr.at[k, way, halves[1 - way]],
            rs1_send.at[slot(k), way, 1],
            rs1_recv.at[k, way, 1],
            step_to[way],
        )

    def rs_on(k, way):
        return remote(
            relay.at[k, way],
            rsr.at[k, way, halves[way]],
            rs2_send.at[slot(k), way],
            rs2_recv.at[k, way],
            step_to[way],
        )

    def z_copy(k, zz):
        return remote(
            zs.at[k],
            zr.at[k, z],
            z_send.at[slot(k), zz],
            z_recv.at[k, z],
            (nxt, zz * XN + x),
        )

    def ag_near(k, way):
        rows = xb.at[k // CHUNKS + 1, chunk_rows(lax.rem(k, CHUNKS)), col(x)]
        return remote(
            rows, rows, ag1_send.at[slot(k), way], ag1_recv.at[k, way], step_to[way]
        )

    def ag_far_rows(k, way, owner):
        return xb.at[k // CHUNKS + 1, chunk_rows(lax.rem(k, CHUNKS), way), col(owner)]

    def ag_far(k, way):
        rows = ag_far_rows(k, way, came_from[way])
        return remote(
            rows, rows, ag2_send.at[slot(k), way], ag2_recv.at[k, way], step_to[way]
        )

    def stage_compute(k):
        w = k // CHUNKS
        c = lax.rem(k, CHUNKS)
        gathered = jnp.logical_or(s == 0, w == 0)

        @pl.when(gathered)
        def _():
            gather_chunk(w, c)

        @pl.when(jnp.logical_not(gathered))
        def _():
            for way in range(2):
                arrived(ag_far_rows(k - CHUNKS, way, at[2]), ag2_recv.at[k - CHUNKS, way])

        project_in(k)

    def stage_attend(k):
        attended = attend(k)

        def project(owner):
            part[k, :, col(owner)] = jnp.dot(
                attended, wo[:, col(owner)], preferred_element_type=jnp.float32
            ).astype(jnp.bfloat16)

        project(at[2])
        for way in range(2):
            rs_through(k, way).start()
        project(at[1])
        rs_near(k, 0).start()
        project(at[3])
        rs_near(k, 1).start()
        project(x)

    def stage_relay(k):
        for way in range(2):
            arrived(relay.at[k, way], rs1_recv.at[k, way, 0])
            relay[k, way] = (
                relay[k, way].astype(jnp.float32)
                + part[k, halves[way], col(at[1 if way == 0 else 3])].astype(jnp.float32)
            ).astype(jnp.bfloat16)
            rs_on(k, way).start()

    def stage_sum(k):
        w = k // CHUNKS
        c = lax.rem(k, CHUNKS)
        for way in range(2):
            arrived(rsr.at[k, way, halves[1 - way]], rs1_recv.at[k, way, 1])
            arrived(rsr.at[k, way, halves[way]], rs2_recv.at[k, way])
        mine = xb[w, chunk_rows(c), col(x)].astype(jnp.float32)
        summed = part[k, :, col(x)].astype(jnp.float32) + jnp.where(z == 0, mine, 0.0)
        summed = summed + rsr[k, 0].astype(jnp.float32) + rsr[k, 1].astype(jnp.float32)
        zs[k] = summed.astype(jnp.bfloat16)

        @pl.when(jnp.logical_and(w < steps - 1, s < sections - 1))
        def _():
            for zz in (1 - z, z):
                z_copy(k, zz).start()

        @pl.when(w == steps - 1)
        def _():
            for h in range(chunk // shard):
                owner = c * (chunk // shard) + h
                rows = pl.ds(h * shard, shard)

                @pl.when(owner == t)
                def _():
                    fin[z, :, col(x)] = zs[k, rows, :]

                @pl.when(owner != t)
                def _():
                    remote(
                        zs.at[k, rows],
                        fin.at[z, :, col(x)],
                        f_send.at[owner],
                        f_recv.at[z, x],
                        (s, owner),
                    ).start()

    def stage_z(k):
        for zz in range(2):
            arrived(zr.at[k, zz], z_recv.at[k, zz])
        xb[k // CHUNKS + 1, chunk_rows(lax.rem(k, CHUNKS)), col(x)] = (
            zr[k, 0].astype(jnp.float32) + zr[k, 1].astype(jnp.float32)
        ).astype(jnp.bfloat16)
        for way in range(2):
            ag_near(k, way).start()

    def stage_forward(k):
        w = k // CHUNKS
        rows = chunk_rows(lax.rem(k, CHUNKS))
        for way in range(2):
            arrived(xb.at[w + 1, rows, col(came_from[way])], ag1_recv.at[k, way])
            ag_far(k, way).start()

    def stage_sent(k):
        for way in range(2):
            for n in range(2):
                sent(relay.at[k, way], rs1_send.at[slot(k), way, n])
            sent(relay.at[k, way], rs2_send.at[slot(k), way])

        @pl.when(jnp.logical_and(k < inner, s < sections - 1))
        def _():
            for zz in range(2):
                sent(zs.at[k], z_send.at[slot(k), zz])

        @pl.when(jnp.logical_and(k < inner, s > 0))
        def _():
            for way in range(2):
                sent(zs.at[k], ag1_send.at[slot(k), way])
                sent(relay.at[k, way], ag2_send.at[slot(k), way])

    @pl.when(z == 0)
    def _():
        gather_across(0, held_ref)

    gather_first(0, held_ref)
    cache_ref[...] = jnp.zeros_like(cache_ref)
    prepare()

    @pl.when(z == 0)
    def _():
        gather_relay(0, 0)

    @pl.when(z == 1)
    def _():
        for u in range(XN):
            relay_unit(0, 0, u)
            z_unit(0, u)
        gather_across(0, held_ref)
        gather_relay(0, 1)

    for copy in loads:
        copy.wait()
    own.wait()

    def body(i, carry):
        def staged(after, count, stage, more=True):
            @pl.when(jnp.logical_and(jnp.logical_and(i >= after, i < after + count), more))
            def _():
                stage(i - after)

        calls = dict(
            compute=(tiles, stage_compute, True),
            attend=(tiles, stage_attend, True),
            relay=(tiles, stage_relay, True),
            sum=(tiles, stage_sum, True),
            z=(inner, stage_z, s > 0),
            forward=(inner, stage_forward, s > 0),
            sent=(tiles, stage_sent, True),
        )
        for name, after in ORDER:
            staged(after, *calls[name])

        entry = jnp.logical_and(s == 0, i < inner)
        w_in = i // CHUNKS
        src = entering_ref.at[w_in]

        @pl.when(jnp.logical_and(entry, lax.rem(i, CHUNKS) == 0))
        def _():
            keep = pltpu.make_async_copy(src, xb.at[w_in + 1, ds(t * shard, shard)], load_sem.at[5])
            keep.start()
            gather_across(w_in + 1, src)
            gather_first(w_in + 1, src)
            keep.wait()

        @pl.when(jnp.logical_and(entry, lax.rem(i, CHUNKS) == CHUNKS // 2))
        def _():
            gather_relay(w_in + 1, 0)
            gather_z(w_in + 1)

        @pl.when(jnp.logical_and(entry, lax.rem(i, CHUNKS) == CHUNKS - 2))
        def _():
            gather_relay(w_in + 1, 1)

        @pl.when(jnp.logical_and(z == 0, i == CHUNKS // 4 - 1))
        def _():
            gather_z(0)

        @pl.when(jnp.logical_and(z == 0, i == CHUNKS // 4))
        def _():
            gather_relay(0, 1)

        return carry

    lax.fori_loop(0, tiles + max(after for _, after in ORDER), body, 0)
    gather_sent(0)

    @pl.when(s == 0)
    def _():
        for w in range(1, steps):
            gather_sent(w)

    for zz in range(2):
        for xx in range(XN):

            @pl.when(zz * XN + xx != t)
            def _():
                arrived(fin.at[zz, :, pl.ds(xx * cols, cols)], f_recv.at[zz, xx])

    leaving_ref[...] = (fin[0].astype(jnp.float32) + fin[1].astype(jnp.float32)).astype(
        jnp.bfloat16
    )
    for owner in range(2 * XN):

        @pl.when(owner != t)
        def _():
            sent(fin.at[0, :, pl.ds(0, cols)], f_send.at[owner])


def shards(
    held_rows,
    entering,
    norm_gain,
    w_query,
    b_query,
    w_keyval,
    b_keyval,
    w_out,
    prefix_keys,
    prefix_values,
    lengths,
):
    sections = lax.axis_size("section")
    _, shard, width = held_rows.shape
    _, steps, prefix, head_dim = prefix_keys.shape
    members = lax.axis_size("tp")
    block = shard * members
    q_cols = w_query.shape[2]
    kv_cols = w_keyval.shape[2]
    q_heads = q_cols // HEAD_DIM
    tiles = steps * CHUNKS
    chunk = block // CHUNKS
    cols = width // XN
    half = HEAD_DIM // 2

    freq = np.exp(-(np.arange(half, dtype=np.float32) * 2.0 / HEAD_DIM) * np.log(ROPE_BASE))
    freq = np.concatenate([freq, freq]).astype(np.float32)
    sign = np.concatenate([-np.ones(half), np.ones(half)]).astype(np.float32)
    angles = np.arange(block, dtype=np.float64)[:, None] * freq[None, :].astype(np.float64)
    freq_sign = np.stack([freq, sign] + [np.zeros_like(freq)] * 6)

    bf16 = jnp.bfloat16
    vmem = pl.BlockSpec(memory_space=pltpu.VMEM)
    hbm = pl.BlockSpec(memory_space=pl.ANY)
    smem = pl.BlockSpec(memory_space=pltpu.SMEM)
    dma = pltpu.SemaphoreType.DMA
    inner = tiles - CHUNKS
    leaving, cache = pl.pallas_call(
        functools.partial(
            relay_kernel, (sections, steps, block, width, shard, q_heads)
        ),
        out_shape=(
            jax.ShapeDtypeStruct((shard, width), bf16),
            jax.ShapeDtypeStruct((steps, block, kv_cols), bf16),
        ),
        in_specs=[smem, hbm, hbm, vmem, hbm, vmem, hbm, vmem, hbm, hbm, hbm, vmem, vmem, vmem],
        out_specs=(vmem, vmem),
        scratch_shapes=[
            pltpu.VMEM((width, q_cols), bf16),
            pltpu.VMEM((width, kv_cols), bf16),
            pltpu.VMEM((q_cols, width), bf16),
            pltpu.VMEM((steps, prefix, head_dim), bf16),
            pltpu.VMEM((steps, prefix, head_dim), bf16),
            pltpu.VMEM((steps, block, width), bf16),
            pltpu.VMEM((tiles, chunk, width), bf16),
            pltpu.VMEM((tiles, 2, chunk // 2, cols), bf16),
            pltpu.VMEM((tiles, 2, chunk, cols), bf16),
            pltpu.VMEM((tiles, chunk, cols), bf16),
            pltpu.VMEM((inner, 2, chunk, cols), bf16),
            pltpu.VMEM((2, shard, width), bf16),
            pltpu.VMEM((2, 8, HEAD_DIM), jnp.float32),
            pltpu.VMEM((q_cols // HEAD_DIM * chunk, HEAD_DIM), bf16),
            dma((6,)),
            dma((steps, XN)),
            dma((steps, XN)),
            dma((steps, 2, XN, 2)),
            dma((steps, 2, XN, 2)),
            dma((steps, 2, XN)),
            dma((steps, 2, XN)),
            dma((SLOTS, 2, 2)),
            dma((tiles, 2, 2)),
            dma((SLOTS, 2)),
            dma((tiles, 2)),
            dma((SLOTS, 2)),
            dma((inner, 2)),
            dma((SLOTS, 2)),
            dma((inner, 2)),
            dma((SLOTS, 2)),
            dma((inner, 2)),
            dma((members,)),
            dma((2, XN)),
        ],
        compiler_params=pltpu.CompilerParams(
            collective_id=0, has_side_effects=True, vmem_limit_bytes=56 * 2**20
        ),
    )(
        lengths,
        held_rows[0],
        entering,
        norm_gain,
        w_query[0],
        b_query,
        w_keyval[0],
        b_keyval,
        w_out[0],
        prefix_keys[0],
        prefix_values[0],
        jnp.asarray(freq_sign, jnp.float32),
        jnp.asarray(np.cos(angles), jnp.float32),
        jnp.asarray(np.sin(angles), jnp.float32),
    )
    return (leaving[None], cache[None])


def solution(mesh):
    return jax.shard_map(
        shards,
        mesh=mesh,
        in_specs=(
            P("section", "tp", None),
            P(None, "tp", None),
            P("section", None),
            P("section", None, "tp"),
            P("section", "tp"),
            P("section", None, "tp"),
            P("section", "tp"),
            P("section", "tp", None),
            P("section", None, None, "tp"),
            P("section", None, None, "tp"),
            P(),
        ),
        out_specs=(P("section", "tp", None), P("section", None, None, "tp")),
        check_vma=False,
    )
```
